512 devices in a mesh: leaf: 16 (over x, y), col: 32 (over z, core).
Axes of the slice: x: 4, y: 4, z: 16, core: 2. Of those that a mesh axis runs over, the one named last changes fastest.
Arguments:
- s_blocks: bfloat16 [1024, 8, 128, 128], P(('leaf', 'col')), may hold values from -0.0059814453 to 0.0059814453
- z_blocks: bfloat16 [1024, 8, 128, 128], P(('leaf', 'col')), may hold values from -1.5 to 1.5
- s_requests: int32 [16, 32, 32, 1], P('leaf', 'col'), may hold values from -1 to 15, as said below
- y_pairs: int32 [1024, 8, 8], P(('leaf', 'col')), may hold values from -1 to 31, as said below
- zt_requests: int32 [16, 32, 32, 1], P('leaf', 'col'), may hold values from -1 to 31, as said below
- d_pairs: int32 [1024, 8, 8], P(('leaf', 'col')), may hold values from -1 to 31, as said below
- d_requests: int32 [16, 32, 32, 1], P('leaf', 'col'), may hold values from -1 to 31, as said below
- e_pairs: int32 [1024, 8, 8], P(('leaf', 'col')), may hold values from -1 to 31, as said below
- z_requests: int32 [16, 32, 32, 1], P('leaf', 'col'), may hold values from -1 to 31, as said below
- z_pairs: int32 [1024, 8, 8], P(('leaf', 'col')), may hold values from -1 to 31, as said below
Outputs:
- z_refined: bfloat16 [1024, 8, 128, 128], P(('leaf', 'col'))
The draws below stay inside these ranges and needn't reach their ends.
Inputs may be any that keep to these rules, and one draw needn't show every extreme that they name: `s_requests`: entry [l, c, p, q] is -1 or a slot of the S holdings of the device (l, p); the entries of one [l, c, p] are distinct. Every reader has some peer with all 1 entries used, and one reader uses all entries. `zt_requests`: entry [l, c, p, q] is -1 or a slot of the Z holdings of the device (l, p); the entries of one [l, c, p] are distinct. Every reader has some peer with all 1 entries used, and one reader uses all entries. `d_requests`: entry [l, c, p, q] is -1 or a slot of the D holdings of the device (l, p); the entries of one [l, c, p] are distinct. Every reader has some peer with all 1 entries used, and one reader uses all entries. `z_requests`: entry [l, c, p, q] is -1 or a slot of the Z holdings of the device (l, p); the entries of one [l, c, p] are distinct. Every reader has some peer with all 1 entries used, and one reader uses all entries. `y_pairs`: each entry is -1 or the position p + q of an entry of s_requests that is not -1, for the reader holding the column; every such entry is named at least once. `d_pairs`: each entry is -1 or the position p + q of an entry of zt_requests that is not -1, for the reader holding the column; every such entry is named at least once. `e_pairs`: each entry is -1 or the position p + q of an entry of d_requests that is not -1, for the reader holding the column; every such entry is named at least once. `z_pairs`: each entry is -1 or the position p + q of an entry of z_requests that is not -1, for the reader holding the column; every such entry is named at least once.
All inputs are finite; a program needn't handle non-finite values.
Results may differ from the reference program's by a relative error of at most 0.0059.
Values may be sent and summed in bfloat16 or wider, within the bound.
No kernel may reach another device: no remote copies, remote signals or barrier semaphores. Data moves between devices by JAX's collectives and lax.ppermute only.
A program may use at most 64 MiB of HBM per device.

```python
import jax
import jax.numpy as jnp
from jax import lax

BLOCK = 128
SLOTS = 8
CAP = 1
CD = 2
NBC = 1024
N_LEAF = 16
N_COL = 32


def request_lists(key, hold_count):
    readers = N_LEAF * N_COL
    fetch_total = N_COL * CAP
    triples = CD * SLOTS * SLOTS
    subkeys = jax.random.split(key, 7)
    reader_load = jax.random.randint(subkeys[0], (readers, 1), 1, 4)
    counts = jnp.minimum(jax.random.randint(subkeys[1], (readers, N_COL), 0, 12) % (reader_load + 1), CAP)
    busy_peer = jax.random.randint(subkeys[2], (readers, 1), 0, N_COL)
    full_reader = jax.random.randint(subkeys[3], (), 0, readers)
    peer_ids = jnp.arange(N_COL)[None, :]
    reader_ids = jnp.arange(readers)[:, None]
    counts = jnp.where((peer_ids == busy_peer) | (reader_ids == full_reader), CAP, counts)
    scores = jax.random.randint(subkeys[4], (readers, N_COL, hold_count), 0, 1 << 20) * hold_count + jnp.arange(hold_count)
    ranked = jnp.argsort(scores, axis=-1)[:, :, :CAP]
    asked_ids = jnp.where(jnp.arange(CAP)[None, None, :] < counts[:, :, None], ranked, -1).astype(jnp.int32)
    live_mask = (asked_ids >= 0).reshape(readers, fetch_total)
    slot_scores = jax.random.randint(subkeys[5], (readers, triples), 0, 1 << 20) * triples + jnp.arange(triples)
    slot_order = jnp.argsort(slot_scores, axis=-1)
    position = jnp.broadcast_to(jnp.arange(triples)[None, :], (readers, triples))
    spare_ids = jax.random.randint(subkeys[6], (readers, triples), 0, fetch_total)
    wanted = jnp.where(position < fetch_total, position, spare_ids)
    wanted_live = jnp.take_along_axis(live_mask, wanted, axis=-1)
    entries = jnp.where(wanted_live, wanted, -1)
    inverse = jnp.argsort(slot_order, axis=-1)
    pair_ids = jnp.take_along_axis(entries, inverse, axis=-1).astype(jnp.int32)
    return (asked_ids.reshape(N_LEAF, N_COL, N_COL, CAP), pair_ids.reshape(NBC, SLOTS, SLOTS))


def draw_s_requests(key, part):
    return request_lists(jax.random.fold_in(key, 11), CD * SLOTS)[0]


def draw_y_pairs(key, part):
    return request_lists(jax.random.fold_in(key, 11), CD * SLOTS)[1]


def draw_zt_requests(key, part):
    return request_lists(jax.random.fold_in(key, 12), 2 * CD * SLOTS)[0]


def draw_d_pairs(key, part):
    return request_lists(jax.random.fold_in(key, 12), 2 * CD * SLOTS)[1]


def draw_d_requests(key, part):
    return request_lists(jax.random.fold_in(key, 13), 2 * CD * SLOTS)[0]


def draw_e_pairs(key, part):
    return request_lists(jax.random.fold_in(key, 13), 2 * CD * SLOTS)[1]


def draw_z_requests(key, part):
    return request_lists(jax.random.fold_in(key, 14), 2 * CD * SLOTS)[0]


def draw_z_pairs(key, part):
    return request_lists(jax.random.fold_in(key, 14), 2 * CD * SLOTS)[1]


def block_levels(stream_key, dims, cuts, smallest, high):
    def one(dim, parts):
        draws = jax.random.uniform(jax.random.fold_in(jax.random.fold_in(stream_key, 6), dim), (parts,), jnp.float32, smallest / len(cuts), high / len(cuts))
        return jnp.repeat(jnp.exp(draws), dims[dim] // parts).reshape((-1,) + (1,) * (len(dims) - dim - 1))

    gain = one(*cuts[0])
    for cut in cuts[1:]:
        gain = gain * one(*cut)
    return gain


def gaussian(stream_key, extent, spread, bound, shards=(), kind=jnp.bfloat16):
    array = spread * jax.random.normal(stream_key, extent, jnp.float32)
    if shards:
        array = array * block_levels(stream_key, extent, shards, -0.22, 0.18)
    return jnp.clip(array, -bound, bound).astype(kind)


def setup_inputs(seed: int = 0) -> dict:
    key_list = jax.random.split(jax.random.key(seed), 11)
    return {
        "s_blocks": gaussian(key_list[0], (NBC, SLOTS, BLOCK, BLOCK), 0.001, 0.0059814453, ((0, 512),)),
        "z_blocks": gaussian(key_list[1], (NBC, SLOTS, BLOCK, BLOCK), 0.25, 1.5, ((0, 512),)),
        "s_requests": draw_s_requests(jax.random.fold_in(key_list[10], 71), 0),
        "y_pairs": draw_y_pairs(jax.random.fold_in(key_list[10], 71), 0),
        "zt_requests": draw_zt_requests(jax.random.fold_in(key_list[10], 71), 0),
        "d_pairs": draw_d_pairs(jax.random.fold_in(key_list[10], 71), 0),
        "d_requests": draw_d_requests(jax.random.fold_in(key_list[10], 71), 0),
        "e_pairs": draw_e_pairs(jax.random.fold_in(key_list[10], 71), 0),
        "z_requests": draw_z_requests(jax.random.fold_in(key_list[10], 71), 0),
        "z_pairs": draw_z_pairs(jax.random.fold_in(key_list[10], 71), 0),
    }


def holdings_of(blocks):
    return blocks.reshape(N_LEAF, N_COL, CD * SLOTS, BLOCK, BLOCK)


def fetch_for(own_blocks, requests, reader):
    hold_count = own_blocks.shape[2]
    leaf_index = reader // N_COL
    partner = leaf_index + 1 - 2 * (leaf_index % 2)
    from_partner = requests >= hold_count
    source_leaf = jnp.where(from_partner, partner, leaf_index).astype(jnp.int32)
    source_slot = jnp.maximum(jnp.where(from_partner, requests - hold_count, requests), 0).astype(jnp.int32)
    peer_ids = jnp.broadcast_to(jnp.arange(N_COL, dtype=jnp.int32)[:, None], requests.shape)
    blocks = own_blocks[source_leaf, peer_ids, source_slot]
    blocks = jnp.where((requests >= 0)[:, :, None, None], blocks, jnp.zeros_like(blocks))
    return blocks.reshape(N_COL * CAP, BLOCK, BLOCK)


def block_products(fetched, pair_ids, local_blocks, flipped):
    fetch_count = fetched.shape[0]
    padded = jnp.concatenate([fetched, jnp.zeros((1,) + fetched.shape[1:], fetched.dtype)], axis=0)
    lookup = jnp.where(pair_ids < 0, fetch_count, pair_ids).astype(jnp.int32)
    chosen = jnp.take(padded, lookup, axis=0).astype(jnp.float32)
    einsum_form = "gabji,gbjk->gaik" if flipped else "gabij,gbjk->gaik"
    return jnp.einsum(einsum_form, chosen, local_blocks.astype(jnp.float32))


def product_pass(own_blocks, requests, pair_ids, local_blocks, flipped):
    readers = N_LEAF * N_COL
    asked_ids = requests.reshape(readers, N_COL, CAP)
    paired = pair_ids.reshape(readers, CD, SLOTS, SLOTS)
    local_rows = local_blocks.reshape(readers, CD, SLOTS, BLOCK, BLOCK)

    def one_reader(packed):
        reader, reader_asks, reader_pairs, reader_local = packed
        fetched = fetch_for(own_blocks, reader_asks, reader)
        return block_products(fetched, reader_pairs, reader_local, flipped)

    result = lax.map(one_reader, (jnp.arange(readers, dtype=jnp.int32), asked_ids, paired, local_rows))
    return result.reshape(NBC, SLOTS, BLOCK, BLOCK)


def reference(s_blocks, z_blocks, s_requests, y_pairs, zt_requests, d_pairs, d_requests, e_pairs, z_requests, z_pairs):
    s_own = holdings_of(s_blocks)
    z_own = holdings_of(z_blocks)
    y_blocks = product_pass(s_own, s_requests, y_pairs, z_blocks, False).astype(jnp.bfloat16)
    first_slot = (jnp.arange(SLOTS) == 0).astype(jnp.float32)
    identity = first_slot[:, None, None] * jnp.eye(BLOCK, dtype=jnp.float32)
    d_blocks = (identity - product_pass(z_own, zt_requests, d_pairs, y_blocks, True)).astype(jnp.bfloat16)
    square = product_pass(holdings_of(d_blocks), d_requests, e_pairs, d_blocks, False)
    e_blocks = (0.5 * d_blocks.astype(jnp.float32) + 0.375 * square).astype(jnp.bfloat16)
    refined = z_blocks.astype(jnp.float32) + product_pass(z_own, z_requests, z_pairs, e_blocks, False)
    return refined.astype(jnp.bfloat16)
```

```python
import functools

import jax
import jax.numpy as jnp
from jax import lax
from jax.experimental import pallas as pl
from jax.experimental.pallas import tpu as pltpu
from jax.sharding import PartitionSpec as P

BF16 = jnp.bfloat16
F32 = jnp.float32
SMEM = pl.BlockSpec(memory_space=pltpu.SMEM)
VMEM = pl.BlockSpec(memory_space=pltpu.VMEM)
ANY = pl.BlockSpec(memory_space=pl.ANY)


def from_partner(value):
    pairs = [(source, source ^ 1) for source in range(lax.axis_size("leaf"))]
    return lax.ppermute(value, "leaf", pairs)


def exchange(value):
    return lax.all_to_all(value, "col", split_axis=0, concat_axis=0, tiled=True)


def pick_kernel(lists, asks, *refs):
    sources = 1 + max(h for _, held in lists for h in held)
    held_refs, out, zero, sem = refs[:sources], refs[sources], refs[-2], refs[-1]
    zero[...] = jnp.zeros_like(zero)
    readers = out.shape[0]

    @pl.loop(0, readers)
    def _(reader):
        for place, (row, held) in enumerate(lists):
            slot = asks[reader, row]
            target = out.at[reader, place]

            @pl.when(slot < 0)
            def _():
                pltpu.make_async_copy(zero, target, sem).start()

            first = 0
            for h in held:
                count = held_refs[h].shape[0]

                @pl.when((slot >= first) & (slot < first + count))
                def _():
                    pltpu.make_async_copy(held_refs[h].at[slot - first], target, sem).start()

                first += count

    pltpu.make_async_copy(out, out, sem).wait()


def pick(asks, holdings, lists, name):
    block = holdings[0].shape[1:]
    shape = (asks.shape[0], len(lists)) + block
    size = 2 * shape[0] * shape[1] * shape[2] * shape[3]
    return pl.pallas_call(
        functools.partial(pick_kernel, lists),
        out_shape=jax.ShapeDtypeStruct(shape, BF16),
        in_specs=[SMEM] + [VMEM] * len(holdings),
        out_specs=ANY,
        scratch_shapes=[pltpu.VMEM(block, BF16), pltpu.SemaphoreType.DMA],
        cost_estimate=pl.CostEstimate(flops=0, bytes_accessed=4 * size, transcendentals=0),
        name=name,
    )(asks, *holdings)


def gather_rows(pairs, blocks, g, wide):
    slots, count = pairs.shape[1], blocks.shape[0] - 1
    size = blocks.shape[1]

    @pl.loop(0, slots)
    def _(a):
        for b in range(slots):
            pair = pairs[g, a, b]
            at = jnp.where(pair < 0, count, pair)
            row = pl.multiple_of(a * size, size)
            wide[pl.ds(row, size), b * size : (b + 1) * size] = blocks[at]


def product(pairs, blocks, g, wide, right):
    gather_rows(pairs, blocks, g, wide)
    tall = right.reshape(right.shape[0] * right.shape[1], right.shape[2])
    return jnp.dot(wide[...], tall, preferred_element_type=F32)


def yd_kernel(y_pairs, d_pairs, fetched, z, d, s_in, zt_in, wide, y, sems):
    count = fetched.shape[0]
    slots, size = z.shape[1], z.shape[2]
    copies = [
        pltpu.make_async_copy(fetched.at[:, i], into.at[pl.ds(0, count)], sems.at[i])
        for i, into in enumerate((s_in, zt_in))
    ]
    for copy in copies:
        copy.start()
    s_in[count] = jnp.zeros((size, size), BF16)
    zt_in[count] = jnp.zeros((size, size), BF16)
    copies[0].wait()
    for g in range(z.shape[0]):
        y[g] = product(y_pairs, s_in, g, wide, z[g]).astype(BF16).reshape(slots, size, size)
    copies[1].wait()

    @pl.loop(0, count)
    def _(i):
        zt_in[i] = zt_in[i].T

    rows = lax.broadcasted_iota(jnp.int32, (slots * size, size), 0)
    columns = lax.broadcasted_iota(jnp.int32, (slots * size, size), 1)
    for g in range(z.shape[0]):
        total = product(d_pairs, zt_in, g, wide, y[g])
        total = jnp.where(rows == columns, 1.0, 0.0) - total
        d[g] = total.astype(BF16).reshape(slots, size, size)


def ez_kernel(e_pairs, z_pairs, d_fetched, z_fetched, d, z, out, d_in, z_in, wide, e, sems):
    count = d_fetched.shape[0]
    slots, size = z.shape[1], z.shape[2]
    copies = [
        pltpu.make_async_copy(src.at[:, 0], into.at[pl.ds(0, count)], sems.at[i])
        for i, (src, into) in enumerate(((d_fetched, d_in), (z_fetched, z_in)))
    ]
    for copy in copies:
        copy.start()
    d_in[count] = jnp.zeros((size, size), BF16)
    z_in[count] = jnp.zeros((size, size), BF16)
    copies[0].wait()
    tall = (slots * size, size)
    for g in range(z.shape[0]):
        square = product(e_pairs, d_in, g, wide, d[g])
        mixed = 0.5 * d[g].reshape(tall).astype(F32) + 0.375 * square
        e[g] = mixed.astype(BF16).reshape(slots, size, size)
    copies[1].wait()
    for g in range(z.shape[0]):
        total = z[g].reshape(tall).astype(F32) + product(z_pairs, z_in, g, wide, e[g])
        out[g] = total.astype(BF16).reshape(slots, size, size)


def paired_call(body, name, pairs, fetched, local):
    columns, slots, size = local[0].shape[:3]
    count = fetched[0].shape[0]
    flops = 4 * columns * slots * slots * size**3
    return pl.pallas_call(
        body,
        out_shape=jax.ShapeDtypeStruct(local[0].shape, BF16),
        in_specs=[SMEM] * 2 + [ANY] * len(fetched) + [VMEM] * len(local),
        out_specs=VMEM,
        scratch_shapes=[
            pltpu.VMEM((count + 1, size, size), BF16),
            pltpu.VMEM((count + 1, size, size), BF16),
            pltpu.VMEM((slots * size, slots * size), BF16),
            pltpu.VMEM(local[0].shape, BF16),
            pltpu.SemaphoreType.DMA((2,)),
        ],
        compiler_params=pltpu.CompilerParams(vmem_limit_bytes=32 * 2**20),
        cost_estimate=pl.CostEstimate(flops=flops, bytes_accessed=16 * 2**20, transcendentals=0),
        name=name,
    )(*pairs, *fetched, *local)


def on_device(
    s_blocks, z_blocks, s_requests, y_pairs, zt_requests, d_pairs, d_requests, e_pairs, z_requests, z_pairs
):
    flat_shape = (-1,) + z_blocks.shape[2:]
    peers = s_requests.shape[2]
    wanted = [r.reshape(peers, 1) for r in (s_requests, zt_requests, z_requests, d_requests)]
    asks = exchange(jnp.concatenate(wanted, axis=1))
    s_own = s_blocks.reshape(flat_shape)
    z_own = z_blocks.reshape(flat_shape)
    z_other = from_partner(z_own)
    first = pick(asks, (s_own, z_own, z_other), ((0, (0,)), (1, (1, 2))), "pick_s_zt")
    second = pick(asks, (z_own, z_other), ((2, (0, 1)),), "pick_z")
    first = exchange(first)
    first, second = lax.optimization_barrier((first, second))
    z_fetched = exchange(second)
    d_blocks = paired_call(yd_kernel, "make_d", (y_pairs, d_pairs), (first,), (z_blocks,))
    d_own = d_blocks.reshape(flat_shape)
    d_other = from_partner(d_own)
    third = pick(asks, (d_own, d_other), ((3, (0, 1)),), "pick_d")
    d_fetched = exchange(third)
    return paired_call(ez_kernel, "refine", (e_pairs, z_pairs), (d_fetched, z_fetched), (d_blocks, z_blocks))


def solution(mesh):
    blocks = P(("leaf", "col"), None, None, None)
    requests = P("leaf", "col", None, None)
    pairs = P(("leaf", "col"), None, None)
    in_specs = (blocks, blocks) + (requests, pairs) * 4
    return jax.shard_map(on_device, mesh=mesh, in_specs=in_specs, out_specs=blocks, check_vma=False)
```

```python
import functools

import jax
import jax.numpy as jnp
from jax import lax
from jax.experimental import pallas as pl
from jax.experimental.pallas import tpu as pltpu
from jax.sharding import PartitionSpec as P

BF16 = jnp.bfloat16
F32 = jnp.float32
SMEM = pl.BlockSpec(memory_space=pltpu.SMEM)
VMEM = pl.BlockSpec(memory_space=pltpu.VMEM)
ANY = pl.BlockSpec(memory_space=pl.ANY)


def from_partner(value):
    pairs = [(source, source ^ 1) for source in range(lax.axis_size("leaf"))]
    return lax.ppermute(value, "leaf", pairs)


def exchange(value):
    return lax.all_to_all(value, "col", split_axis=0, concat_axis=0, tiled=True)


def pick_kernel(lists, asks, *refs):
    sources = max(end for _, _, end in lists)
    held, out = refs[:sources], refs[sources]
    stores, asked, sem, in_sems = refs[sources + 1 : -3], refs[-3], refs[-2], refs[-1]
    readers = out.shape[0]
    ask_copy = pltpu.make_async_copy(asks, asked, in_sems.at[in_sems.shape[0] - 1])
    ask_copy.start()
    copies, sizes = [], []
    for store, (_, begin, end) in zip(stores, lists):
        first = 0
        for h in range(begin, end):
            count = held[h].shape[0]
            copies.append(pltpu.make_async_copy(held[h], store.at[pl.ds(first, count)], in_sems.at[len(copies)]))
            first += count
        sizes.append(first)
    for copy in copies:
        copy.start()
    for store, size in zip(stores, sizes):
        store[size] = jnp.zeros(store.shape[1:], BF16)
    ask_copy.wait()
    for copy in copies:
        copy.wait()

    @pl.loop(0, readers)
    def _(reader):
        for place, (store, size, (row, _, _)) in enumerate(zip(stores, sizes, lists)):
            slot = asked[reader, row]
            at = jnp.where(slot < 0, size, slot)
            pltpu.make_async_copy(store.at[at], out.at[reader, place], sem).start()

    pltpu.make_async_copy(out, out, sem).wait()


def pick(asks, holdings, lists, name):
    block = holdings[0].shape[1:]
    shape = (asks.shape[0], len(lists)) + block
    size = 2 * shape[0] * shape[1] * shape[2] * shape[3]
    stores = [
        pltpu.VMEM((1 + sum(h.shape[0] for h in holdings[begin:end]),) + block, BF16) for _, begin, end in lists
    ]
    return pl.pallas_call(
        functools.partial(pick_kernel, lists),
        out_shape=jax.ShapeDtypeStruct(shape, BF16),
        in_specs=[ANY] * (1 + len(holdings)),
        out_specs=ANY,
        scratch_shapes=[
            *stores,
            pltpu.SMEM(asks.shape, jnp.int32),
            pltpu.SemaphoreType.DMA,
            pltpu.SemaphoreType.DMA((1 + sum(end - begin for _, begin, end in lists),)),
        ],
        cost_estimate=pl.CostEstimate(flops=0, bytes_accessed=3 * size, transcendentals=0),
        name=name,
    )(asks, *holdings)


def product(pairs, blocks, g, a, right):
    slots, last = pairs.shape[2], blocks.shape[0] - 1
    chosen = []
    for b in range(slots):
        pair = pairs[g, a, b]
        chosen.append(blocks[jnp.where(pair < 0, last, pair)])
    tall = right.reshape(right.shape[0] * right.shape[1], right.shape[2])
    return jnp.dot(jnp.concatenate(chosen, axis=1), tall, preferred_element_type=F32)


def yd_kernel(at, y_pairs, d_pairs, fetched, z, d, s_in, zt_in, y, sems):
    count = fetched.shape[0]
    columns, slots, size = z.shape[:3]
    copies = [
        pltpu.make_async_copy(fetched.at[:, i], into.at[pl.ds(0, count)], sems.at[i])
        for i, into in zip(at, (s_in, zt_in))
    ]
    for copy in copies:
        copy.start()
    s_in[count] = jnp.zeros((size, size), BF16)
    zt_in[count] = jnp.zeros((size, size), BF16)
    copies[0].wait()
    for g in range(columns):
        for a in range(slots):
            y[g, a] = product(y_pairs, s_in, g, a, z[g]).astype(BF16)
    copies[1].wait()

    @pl.loop(0, count)
    def _(i):
        zt_in[i] = zt_in[i].T

    rows = lax.broadcasted_iota(jnp.int32, (size, size), 0)
    identity = jnp.where(rows == lax.broadcasted_iota(jnp.int32, (size, size), 1), 1.0, 0.0)
    for g in range(columns):
        for a in range(slots):
            total = product(d_pairs, zt_in, g, a, y[g])
            d[g, a] = (identity - total if a == 0 else -total).astype(BF16)


def ez_kernel(at, e_pairs, z_pairs, d_fetched, z_fetched, d, z, out, d_in, z_in, e, sems):
    count = d_fetched.shape[0]
    columns, slots, size = z.shape[:3]
    copies = [
        pltpu.make_async_copy(src.at[:, i], into.at[pl.ds(0, count)], sems.at[k])
        for k, (i, src, into) in enumerate(zip(at, (d_fetched, z_fetched), (d_in, z_in)))
    ]
    for copy in copies:
        copy.start()
    d_in[count] = jnp.zeros((size, size), BF16)
    z_in[count] = jnp.zeros((size, size), BF16)
    copies[0].wait()
    for g in range(columns):
        for a in range(slots):
            square = product(e_pairs, d_in, g, a, d[g])
            e[g, a] = (0.5 * d[g, a].astype(F32) + 0.375 * square).astype(BF16)
    copies[1].wait()
    for g in range(columns):
        for a in range(slots):
            total = z[g, a].astype(F32) + product(z_pairs, z_in, g, a, e[g])
            out[g, a] = total.astype(BF16)


def paired_call(body, name, pairs, fetched, local):
    columns, slots, size = local[0].shape[:3]
    count = fetched[0].shape[0]
    flops = 4 * columns * slots * slots * size**3
    return pl.pallas_call(
        body,
        out_shape=jax.ShapeDtypeStruct(local[0].shape, BF16),
        in_specs=[SMEM] * 2 + [ANY] * len(fetched) + [VMEM] * len(local),
        out_specs=VMEM,
        scratch_shapes=[
            pltpu.VMEM((count + 1, size, size), BF16),
            pltpu.VMEM((count + 1, size, size), BF16),
            pltpu.VMEM(local[0].shape, BF16),
            pltpu.SemaphoreType.DMA((2,)),
        ],
        compiler_params=pltpu.CompilerParams(vmem_limit_bytes=32 * 2**20),
        cost_estimate=pl.CostEstimate(flops=flops, bytes_accessed=16 * 2**20, transcendentals=0),
        name=name,
    )(*pairs, *fetched, *local)


def on_device(
    s_blocks, z_blocks, s_requests, y_pairs, zt_requests, d_pairs, d_requests, e_pairs, z_requests, z_pairs
):
    flat_shape = (-1,) + z_blocks.shape[2:]
    peers = s_requests.shape[2]
    wanted = [r.reshape(peers, 1) for r in (s_requests, zt_requests, z_requests, d_requests)]
    asks = exchange(jnp.concatenate(wanted, axis=1))
    s_own = s_blocks.reshape(flat_shape)
    z_own = z_blocks.reshape(flat_shape)
    z_other = from_partner(z_own)
    first = pick(asks, (s_own, z_own, z_other), ((0, 0, 1), (1, 1, 3)), "pick_s_zt")
    second = pick(asks, (z_own, z_other), ((2, 0, 2),), "pick_z")
    first = exchange(first)
    first, second = lax.optimization_barrier((first, second))
    z_fetched = exchange(second)
    make_d = functools.partial(yd_kernel, (0, 1))
    d_blocks = paired_call(make_d, "make_d", (y_pairs, d_pairs), (first,), (z_blocks,))
    d_own = d_blocks.reshape(flat_shape)
    d_other = from_partner(d_own)
    third = pick(asks, (d_own, d_other), ((3, 0, 2),), "pick_d")
    d_fetched = exchange(third)
    refine = functools.partial(ez_kernel, (0, 0))
    return paired_call(refine, "refine", (e_pairs, z_pairs), (d_fetched, z_fetched), (d_blocks, z_blocks))


def solution(mesh):
    blocks = P(("leaf", "col"), None, None, None)
    requests = P("leaf", "col", None, None)
    pairs = P(("leaf", "col"), None, None)
    in_specs = (blocks, blocks) + (requests, pairs) * 4
    return jax.shard_map(on_device, mesh=mesh, in_specs=in_specs, out_specs=blocks, check_vma=False)
```

```python
import functools

import jax
import jax.numpy as jnp
from jax import lax
from jax.experimental import pallas as pl
from jax.experimental.pallas import tpu as pltpu
from jax.sharding import PartitionSpec as P

BF16 = jnp.bfloat16
F32 = jnp.float32
SMEM = pl.BlockSpec(memory_space=pltpu.SMEM)
VMEM = pl.BlockSpec(memory_space=pltpu.VMEM)
ANY = pl.BlockSpec(memory_space=pl.ANY)


def from_partner(value):
    pairs = [(source, source ^ 1) for source in range(lax.axis_size("leaf"))]
    return lax.ppermute(value, "leaf", pairs)


def standing(peer, count):
    return (count // 2 + 1 - peer + count) % count


def exchange(value):
    count = lax.axis_size("col")
    group = sorted(range(count), key=lambda peer: standing(peer, count))
    return lax.all_to_all(value, "col", 0, 0, axis_index_groups=[group], tiled=True)


def exchange_asks(asks):
    count = asks.shape[0]
    group = [(row + count // 2) % count for row in range(count)]
    asks = jnp.roll(asks, -(count // 2), axis=0)
    return lax.all_to_all(asks, "col", 0, 0, axis_index_groups=[group], tiled=True)


def asks_row(place, count):
    return lax.rem(count + 1 - place, count)


def pick_kernel(lists, asks, *refs):
    sources = max(end for _, _, end in lists)
    held, out = refs[:sources], refs[sources]
    stores, asked, sem, in_sems = refs[sources + 1 : -3], refs[-3], refs[-2], refs[-1]
    readers = out.shape[0]
    ask_copy = pltpu.make_async_copy(asks, asked, in_sems.at[in_sems.shape[0] - 1])
    ask_copy.start()
    copies, sizes = [], []
    for store, (_, begin, end) in zip(stores, lists):
        first = 0
        for h in range(begin, end):
            count = held[h].shape[0]
            copies.append(pltpu.make_async_copy(held[h], store.at[pl.ds(first, count)], in_sems.at[len(copies)]))
            first += count
        sizes.append(first)
    for copy in copies:
        copy.start()
    for store, size in zip(stores, sizes):
        store[size] = jnp.zeros(store.shape[1:], BF16)
    ask_copy.wait()
    for copy in copies:
        copy.wait()

    @pl.loop(0, readers)
    def _(reader):
        for place, (store, size, (row, _, _)) in enumerate(zip(stores, sizes, lists)):
            slot = asked[asks_row(reader, readers), row]
            at = jnp.where(slot < 0, size, slot)
            pltpu.make_async_copy(store.at[at], out.at[reader, place], sem).start()

    pltpu.make_async_copy(out, out, sem).wait()


def pick(asks, holdings, lists, name):
    block = holdings[0].shape[1:]
    shape = (asks.shape[0], len(lists)) + block
    size = 2 * shape[0] * shape[1] * shape[2] * shape[3]
    stores = [
        pltpu.VMEM((1 + sum(h.shape[0] for h in holdings[begin:end]),) + block, BF16) for _, begin, end in lists
    ]
    return pl.pallas_call(
        functools.partial(pick_kernel, lists),
        out_shape=jax.ShapeDtypeStruct(shape, BF16),
        in_specs=[ANY] * (1 + len(holdings)),
        out_specs=ANY,
        scratch_shapes=[
            *stores,
            pltpu.SMEM(asks.shape, jnp.int32),
            pltpu.SemaphoreType.DMA,
            pltpu.SemaphoreType.DMA((1 + sum(end - begin for _, begin, end in lists),)),
        ],
        cost_estimate=pl.CostEstimate(flops=0, bytes_accessed=3 * size, transcendentals=0),
        name=name,
    )(asks, *holdings)


def product(pairs, blocks, g, a, right):
    chosen = [blocks[pairs[g, a, b]] for b in range(pairs.shape[2])]
    tall = right.reshape(right.shape[0] * right.shape[1], right.shape[2])
    return jnp.dot(jnp.concatenate(chosen, axis=1), tall, preferred_element_type=F32)


def yd_kernel(at, y_pairs, d_pairs, fetched, z, d, s_in, zt_in, y, sems):
    count = fetched.shape[0]
    columns, slots, size = z.shape[:3]
    copies = [
        pltpu.make_async_copy(fetched.at[:, i], into.at[pl.ds(0, count)], sems.at[i])
        for i, into in zip(at, (s_in, zt_in))
    ]
    for copy in copies:
        copy.start()
    s_in[count] = jnp.zeros((size, size), BF16)
    zt_in[count] = jnp.zeros((size, size), BF16)
    copies[0].wait()
    for g in range(columns):
        for a in range(slots):
            y[g, a] = product(y_pairs, s_in, g, a, z[g]).astype(BF16)
    copies[1].wait()

    @pl.loop(0, count)
    def _(i):
        zt_in[i] = zt_in[i].T

    rows = lax.broadcasted_iota(jnp.int32, (size, size), 0)
    identity = jnp.where(rows == lax.broadcasted_iota(jnp.int32, (size, size), 1), 1.0, 0.0)
    for g in range(columns):
        for a in range(slots):
            total = product(d_pairs, zt_in, g, a, y[g])
            d[g, a] = (identity - total if a == 0 else -total).astype(BF16)


def ez_kernel(at, e_pairs, z_pairs, d_fetched, z_fetched, d, z, out, d_in, z_in, e, sems):
    count = d_fetched.shape[0]
    columns, slots, size = z.shape[:3]
    copies = [
        pltpu.make_async_copy(src.at[:, i], into.at[pl.ds(0, count)], sems.at[k])
        for k, (i, src, into) in enumerate(zip(at, (d_fetched, z_fetched), (d_in, z_in)))
    ]
    for copy in copies:
        copy.start()
    d_in[count] = jnp.zeros((size, size), BF16)
    z_in[count] = jnp.zeros((size, size), BF16)
    copies[0].wait()
    for g in range(columns):
        for a in range(slots):
            square = product(e_pairs, d_in, g, a, d[g])
            e[g, a] = (0.5 * d[g, a].astype(F32) + 0.375 * square).astype(BF16)
    copies[1].wait()
    for g in range(columns):
        for a in range(slots):
            total = z[g, a].astype(F32) + product(z_pairs, z_in, g, a, e[g])
            out[g, a] = total.astype(BF16)


def paired_call(body, name, pairs, fetched, local):
    columns, slots, size = local[0].shape[:3]
    count = fetched[0].shape[0]
    flops = 4 * columns * slots * slots * size**3
    return pl.pallas_call(
        body,
        out_shape=jax.ShapeDtypeStruct(local[0].shape, BF16),
        in_specs=[SMEM] * 2 + [ANY] * len(fetched) + [VMEM] * len(local),
        out_specs=VMEM,
        scratch_shapes=[
            pltpu.VMEM((count + 1, size, size), BF16),
            pltpu.VMEM((count + 1, size, size), BF16),
            pltpu.VMEM(local[0].shape, BF16),
            pltpu.SemaphoreType.DMA((2,)),
        ],
        compiler_params=pltpu.CompilerParams(vmem_limit_bytes=32 * 2**20),
        cost_estimate=pl.CostEstimate(flops=flops, bytes_accessed=16 * 2**20, transcendentals=0),
        name=name,
    )(*pairs, *fetched, *local)


def on_device(
    s_blocks, z_blocks, s_requests, y_pairs, zt_requests, d_pairs, d_requests, e_pairs, z_requests, z_pairs
):
    flat_shape = (-1,) + z_blocks.shape[2:]
    peers = s_requests.shape[2]
    wanted = [r.reshape(peers, 1) for r in (s_requests, zt_requests, z_requests, d_requests)]
    asks = exchange_asks(jnp.concatenate(wanted, axis=1))
    pairs = [
        jnp.where(pair < 0, peers, standing(jnp.maximum(pair, 0), peers)) for pair in (y_pairs, d_pairs, e_pairs, z_pairs)
    ]
    s_own = s_blocks.reshape(flat_shape)
    z_own = z_blocks.reshape(flat_shape)
    z_other = from_partner(z_own)
    first = pick(asks, (s_own, z_own, z_other), ((0, 0, 1), (1, 1, 3)), "pick_s_zt")
    second = pick(asks, (z_own, z_other), ((2, 0, 2),), "pick_z")
    first = exchange(first)
    first, second = lax.optimization_barrier((first, second))
    z_fetched = exchange(second)
    make_d = functools.partial(yd_kernel, (0, 1))
    d_blocks = paired_call(make_d, "make_d", pairs[:2], (first,), (z_blocks,))
    d_own = d_blocks.reshape(flat_shape)
    d_other = from_partner(d_own)
    third = pick(asks, (d_own, d_other), ((3, 0, 2),), "pick_d")
    d_fetched = exchange(third)
    refine = functools.partial(ez_kernel, (0, 0))
    return paired_call(refine, "refine", pairs[2:], (d_fetched, z_fetched), (d_blocks, z_blocks))


def solution(mesh):
    blocks = P(("leaf", "col"), None, None, None)
    requests = P("leaf", "col", None, None)
    pairs = P(("leaf", "col"), None, None)
    in_specs = (blocks, blocks) + (requests, pairs) * 4
    return jax.shard_map(on_device, mesh=mesh, in_specs=in_specs, out_specs=blocks, check_vma=False)
```

```python
import functools

import jax
import jax.numpy as jnp
from jax import lax
from jax.experimental import pallas as pl
from jax.experimental.pallas import tpu as pltpu
from jax.sharding import PartitionSpec as P

BF16 = jnp.bfloat16
F32 = jnp.float32
SMEM = pl.BlockSpec(memory_space=pltpu.SMEM)
VMEM = pl.BlockSpec(memory_space=pltpu.VMEM)
ANY = pl.BlockSpec(memory_space=pl.ANY)


def from_partner(value):
    pairs = [(source, source ^ 1) for source in range(lax.axis_size("leaf"))]
    return lax.ppermute(value, "leaf", pairs)


def first_of(count):
    return count // 2 + 1


def standing(peer, count):
    return (first_of(count) - peer + count) % count


def exchange(value):
    count = lax.axis_size("col")
    group = sorted(range(count), key=lambda peer: standing(peer, count))
    return lax.all_to_all(value, "col", 0, 0, axis_index_groups=[group], tiled=True)


def turned(count):
    return 2 * (count // 3) + 2


def exchange_asks(asks):
    count = asks.shape[0]
    group = [(row + turned(count)) % count for row in range(count)]
    asks = jnp.roll(asks, -turned(count), axis=0)
    return lax.all_to_all(asks, "col", 0, 0, axis_index_groups=[group], tiled=True)


def asks_row(place, count):
    row = (first_of(count) - turned(count)) % count - place
    return jnp.where(row < 0, row + count, row)


def pick_kernel(lists, asks, *refs):
    sources = max(end for _, _, end in lists)
    held, out = refs[:sources], refs[sources]
    stores, asked, sem, in_sems = refs[sources + 1 : -3], refs[-3], refs[-2], refs[-1]
    readers = out.shape[0]
    ask_copy = pltpu.make_async_copy(asks, asked, in_sems.at[in_sems.shape[0] - 1])
    ask_copy.start()
    copies, sizes = [], []
    for store, (_, begin, end) in zip(stores, lists):
        first = 0
        for h in range(begin, end):
            count = held[h].shape[0]
            copies.append(pltpu.make_async_copy(held[h], store.at[pl.ds(first, count)], in_sems.at[len(copies)]))
            first += count
        sizes.append(first)
    for copy in copies:
        copy.start()
    for store, size in zip(stores, sizes):
        store[size] = jnp.zeros(store.shape[1:], BF16)
    ask_copy.wait()
    for copy in copies:
        copy.wait()

    @pl.loop(0, readers)
    def _(reader):
        for place, (store, size, (row, _, _)) in enumerate(zip(stores, sizes, lists)):
            slot = asked[asks_row(reader, readers), row]
            at = jnp.where(slot < 0, size, slot)
            pltpu.make_async_copy(store.at[at], out.at[reader, place], sem).start()

    pltpu.make_async_copy(out, out, sem).wait()


def pick(asks, holdings, lists, name):
    block = holdings[0].shape[1:]
    shape = (asks.shape[0], len(lists)) + block
    size = 2 * shape[0] * shape[1] * shape[2] * shape[3]
    stores = [
        pltpu.VMEM((1 + sum(h.shape[0] for h in holdings[begin:end]),) + block, BF16) for _, begin, end in lists
    ]
    return pl.pallas_call(
        functools.partial(pick_kernel, lists),
        out_shape=jax.ShapeDtypeStruct(shape, BF16),
        in_specs=[ANY] * (1 + len(holdings)),
        out_specs=ANY,
        scratch_shapes=[
            *stores,
            pltpu.SMEM(asks.shape, jnp.int32),
            pltpu.SemaphoreType.DMA,
            pltpu.SemaphoreType.DMA((1 + sum(end - begin for _, begin, end in lists),)),
        ],
        cost_estimate=pl.CostEstimate(flops=0, bytes_accessed=3 * size, transcendentals=0),
        name=name,
    )(asks, *holdings)


def product(pairs, blocks, g, a, right):
    chosen = [blocks[pairs[g, a, b]] for b in range(pairs.shape[2])]
    tall = right.reshape(right.shape[0] * right.shape[1], right.shape[2])
    return jnp.dot(jnp.concatenate(chosen, axis=1), tall, preferred_element_type=F32)


def yd_kernel(at, y_pairs, d_pairs, fetched, z, d, s_in, zt_in, y, sems):
    count = fetched.shape[0]
    columns, slots, size = z.shape[:3]
    copies = [
        pltpu.make_async_copy(fetched.at[:, i], into.at[pl.ds(0, count)], sems.at[i])
        for i, into in zip(at, (s_in, zt_in))
    ]
    for copy in copies:
        copy.start()
    s_in[count] = jnp.zeros((size, size), BF16)
    zt_in[count] = jnp.zeros((size, size), BF16)
    copies[0].wait()
    for g in range(columns):
        for a in range(slots):
            y[g, a] = product(y_pairs, s_in, g, a, z[g]).astype(BF16)
    copies[1].wait()

    @pl.loop(0, count)
    def _(i):
        zt_in[i] = zt_in[i].T

    rows = lax.broadcasted_iota(jnp.int32, (size, size), 0)
    identity = jnp.where(rows == lax.broadcasted_iota(jnp.int32, (size, size), 1), 1.0, 0.0)
    for g in range(columns):
        for a in range(slots):
            total = product(d_pairs, zt_in, g, a, y[g])
            d[g, a] = (identity - total if a == 0 else -total).astype(BF16)


def ez_kernel(at, e_pairs, z_pairs, d_fetched, z_fetched, d, z, out, d_in, z_in, e, sems):
    count = d_fetched.shape[0]
    columns, slots, size = z.shape[:3]
    copies = [
        pltpu.make_async_copy(src.at[:, i], into.at[pl.ds(0, count)], sems.at[k])
        for k, (i, src, into) in enumerate(zip(at, (d_fetched, z_fetched), (d_in, z_in)))
    ]
    for copy in copies:
        copy.start()
    d_in[count] = jnp.zeros((size, size), BF16)
    z_in[count] = jnp.zeros((size, size), BF16)
    copies[0].wait()
    for g in range(columns):
        for a in range(slots):
            square = product(e_pairs, d_in, g, a, d[g])
            e[g, a] = (0.5 * d[g, a].astype(F32) + 0.375 * square).astype(BF16)
    copies[1].wait()
    for g in range(columns):
        for a in range(slots):
            total = z[g, a].astype(F32) + product(z_pairs, z_in, g, a, e[g])
            out[g, a] = total.astype(BF16)


def paired_call(body, name, pairs, fetched, local):
    columns, slots, size = local[0].shape[:3]
    count = fetched[0].shape[0]
    flops = 4 * columns * slots * slots * size**3
    return pl.pallas_call(
        body,
        out_shape=jax.ShapeDtypeStruct(local[0].shape, BF16),
        in_specs=[SMEM] * 2 + [ANY] * len(fetched) + [VMEM] * len(local),
        out_specs=VMEM,
        scratch_shapes=[
            pltpu.VMEM((count + 1, size, size), BF16),
            pltpu.VMEM((count + 1, size, size), BF16),
            pltpu.VMEM(local[0].shape, BF16),
            pltpu.SemaphoreType.DMA((2,)),
        ],
        compiler_params=pltpu.CompilerParams(vmem_limit_bytes=32 * 2**20),
        cost_estimate=pl.CostEstimate(flops=flops, bytes_accessed=16 * 2**20, transcendentals=0),
        name=name,
    )(*pairs, *fetched, *local)


def on_device(
    s_blocks, z_blocks, s_requests, y_pairs, zt_requests, d_pairs, d_requests, e_pairs, z_requests, z_pairs
):
    flat_shape = (-1,) + z_blocks.shape[2:]
    peers = s_requests.shape[2]
    wanted = [r.reshape(peers, 1) for r in (s_requests, zt_requests, z_requests, d_requests)]
    asks = exchange_asks(jnp.concatenate(wanted, axis=1))
    pairs = [
        jnp.where(pair < 0, peers, standing(jnp.maximum(pair, 0), peers)) for pair in (y_pairs, d_pairs, e_pairs, z_pairs)
    ]
    s_own = s_blocks.reshape(flat_shape)
    z_own = z_blocks.reshape(flat_shape)
    z_other = from_partner(z_own)
    first = pick(asks, (s_own, z_own, z_other), ((0, 0, 1), (1, 1, 3)), "pick_s_zt")
    second = pick(asks, (z_own, z_other), ((2, 0, 2),), "pick_z")
    first = exchange(first)
    first, second = lax.optimization_barrier((first, second))
    z_fetched = exchange(second)
    make_d = functools.partial(yd_kernel, (0, 1))
    d_blocks = paired_call(make_d, "make_d", pairs[:2], (first,), (z_blocks,))
    d_own = d_blocks.reshape(flat_shape)
    d_other = from_partner(d_own)
    third = pick(asks, (d_own, d_other), ((3, 0, 2),), "pick_d")
    d_fetched = exchange(third)
    refine = functools.partial(ez_kernel, (0, 0))
    return paired_call(refine, "refine", pairs[2:], (d_fetched, z_fetched), (d_blocks, z_blocks))


def solution(mesh):
    blocks = P(("leaf", "col"), None, None, None)
    requests = P("leaf", "col", None, None)
    pairs = P(("leaf", "col"), None, None)
    in_specs = (blocks, blocks) + (requests, pairs) * 4
    return jax.shard_map(on_device, mesh=mesh, in_specs=in_specs, out_specs=blocks, check_vma=False)
```

```python
import functools

import jax
import jax.numpy as jnp
from jax import lax
from jax.experimental import pallas as pl
from jax.experimental.pallas import tpu as pltpu
from jax.sharding import PartitionSpec as P

BF16 = jnp.bfloat16
F32 = jnp.float32
SMEM = pl.BlockSpec(memory_space=pltpu.SMEM)
VMEM = pl.BlockSpec(memory_space=pltpu.VMEM)
ANY = pl.BlockSpec(memory_space=pl.ANY)


def from_partner(value):
    pairs = [(source, source ^ 1) for source in range(lax.axis_size("leaf"))]
    return lax.ppermute(value, "leaf", pairs)


def first_of(count):
    return count // 2 + 5


def standing(peer, count):
    return (first_of(count) - peer + count) % count


def exchange(value):
    count = lax.axis_size("col")
    group = sorted(range(count), key=lambda peer: standing(peer, count))
    return lax.all_to_all(value, "col", 0, 0, axis_index_groups=[group], tiled=True)


def turned(count):
    return 2 * (count // 3) + 2


def exchange_asks(asks):
    count = asks.shape[0]
    group = [(row + turned(count)) % count for row in range(count)]
    asks = jnp.roll(asks, -turned(count), axis=0)
    return lax.all_to_all(asks, "col", 0, 0, axis_index_groups=[group], tiled=True)


def asks_row(place, count):
    row = (first_of(count) - turned(count)) % count - place
    return jnp.where(row < 0, row + count, row)


def pick_kernel(lists, asks, *refs):
    sources = max(end for _, _, end in lists)
    held, out = refs[:sources], refs[sources]
    stores, asked, sem, in_sems = refs[sources + 1 : -3], refs[-3], refs[-2], refs[-1]
    readers = out.shape[0]
    ask_copy = pltpu.make_async_copy(asks, asked, in_sems.at[in_sems.shape[0] - 1])
    ask_copy.start()
    copies, sizes = [], []
    for store, (_, begin, end) in zip(stores, lists):
        first = 0
        for h in range(begin, end):
            count = held[h].shape[0]
            copies.append(pltpu.make_async_copy(held[h], store.at[pl.ds(first, count)], in_sems.at[len(copies)]))
            first += count
        sizes.append(first)
    for copy in copies:
        copy.start()
    for store, size in zip(stores, sizes):
        store[size] = jnp.zeros(store.shape[1:], BF16)
    ask_copy.wait()
    for copy in copies:
        copy.wait()

    @pl.loop(0, readers)
    def _(reader):
        for place, (store, size, (row, _, _)) in enumerate(zip(stores, sizes, lists)):
            slot = asked[asks_row(reader, readers), row]
            at = jnp.where(slot < 0, size, slot)
            pltpu.make_async_copy(store.at[at], out.at[reader, place], sem).start()

    pltpu.make_async_copy(out, out, sem).wait()


def pick(asks, holdings, lists, name):
    block = holdings[0].shape[1:]
    shape = (asks.shape[0], len(lists)) + block
    size = 2 * shape[0] * shape[1] * shape[2] * shape[3]
    stores = [
        pltpu.VMEM((1 + sum(h.shape[0] for h in holdings[begin:end]),) + block, BF16) for _, begin, end in lists
    ]
    return pl.pallas_call(
        functools.partial(pick_kernel, lists),
        out_shape=jax.ShapeDtypeStruct(shape, BF16),
        in_specs=[ANY] * (1 + len(holdings)),
        out_specs=ANY,
        scratch_shapes=[
            *stores,
            pltpu.SMEM(asks.shape, jnp.int32),
            pltpu.SemaphoreType.DMA,
            pltpu.SemaphoreType.DMA((1 + sum(end - begin for _, begin, end in lists),)),
        ],
        cost_estimate=pl.CostEstimate(flops=0, bytes_accessed=3 * size, transcendentals=0),
        name=name,
    )(asks, *holdings)


def product(pairs, blocks, g, a, right):
    chosen = [blocks[pairs[g, a, b]] for b in range(pairs.shape[2])]
    tall = right.reshape(right.shape[0] * right.shape[1], right.shape[2])
    return jnp.dot(jnp.concatenate(chosen, axis=1), tall, preferred_element_type=F32)


def yd_kernel(at, y_pairs, d_pairs, fetched, z, d, s_in, zt_in, y, sems):
    count = fetched.shape[0]
    columns, slots, size = z.shape[:3]
    copies = [
        pltpu.make_async_copy(fetched.at[:, i], into.at[pl.ds(0, count)], sems.at[i])
        for i, into in zip(at, (s_in, zt_in))
    ]
    for copy in copies:
        copy.start()
    s_in[count] = jnp.zeros((size, size), BF16)
    zt_in[count] = jnp.zeros((size, size), BF16)
    copies[0].wait()
    for g in range(columns):
        for a in range(slots):
            y[g, a] = product(y_pairs, s_in, g, a, z[g]).astype(BF16)
    copies[1].wait()

    @pl.loop(0, count)
    def _(i):
        zt_in[i] = zt_in[i].T

    rows = lax.broadcasted_iota(jnp.int32, (size, size), 0)
    identity = jnp.where(rows == lax.broadcasted_iota(jnp.int32, (size, size), 1), 1.0, 0.0)
    for g in range(columns):
        for a in range(slots):
            total = product(d_pairs, zt_in, g, a, y[g])
            d[g, a] = (identity - total if a == 0 else -total).astype(BF16)


def ez_kernel(at, e_pairs, z_pairs, d_fetched, z_fetched, d, z, out, d_in, z_in, e, sems):
    count = d_fetched.shape[0]
    columns, slots, size = z.shape[:3]
    copies = [
        pltpu.make_async_copy(src.at[:, i], into.at[pl.ds(0, count)], sems.at[k])
        for k, (i, src, into) in enumerate(zip(at, (d_fetched, z_fetched), (d_in, z_in)))
    ]
    for copy in copies:
        copy.start()
    d_in[count] = jnp.zeros((size, size), BF16)
    z_in[count] = jnp.zeros((size, size), BF16)
    copies[0].wait()
    for g in range(columns):
        for a in range(slots):
            square = product(e_pairs, d_in, g, a, d[g])
            e[g, a] = (0.5 * d[g, a].astype(F32) + 0.375 * square).astype(BF16)
    copies[1].wait()
    for g in range(columns):
        for a in range(slots):
            total = z[g, a].astype(F32) + product(z_pairs, z_in, g, a, e[g])
            out[g, a] = total.astype(BF16)


def paired_call(body, name, pairs, fetched, local):
    columns, slots, size = local[0].shape[:3]
    count = fetched[0].shape[0]
    flops = 4 * columns * slots * slots * size**3
    return pl.pallas_call(
        body,
        out_shape=jax.ShapeDtypeStruct(local[0].shape, BF16),
        in_specs=[SMEM] * 2 + [ANY] * len(fetched) + [VMEM] * len(local),
        out_specs=VMEM,
        scratch_shapes=[
            pltpu.VMEM((count + 1, size, size), BF16),
            pltpu.VMEM((count + 1, size, size), BF16),
            pltpu.VMEM(local[0].shape, BF16),
            pltpu.SemaphoreType.DMA((2,)),
        ],
        compiler_params=pltpu.CompilerParams(vmem_limit_bytes=32 * 2**20),
        cost_estimate=pl.CostEstimate(flops=flops, bytes_accessed=16 * 2**20, transcendentals=0),
        name=name,
    )(*pairs, *fetched, *local)


def on_device(
    s_blocks, z_blocks, s_requests, y_pairs, zt_requests, d_pairs, d_requests, e_pairs, z_requests, z_pairs
):
    flat_shape = (-1,) + z_blocks.shape[2:]
    peers = s_requests.shape[2]
    wanted = [r.reshape(peers, 1) for r in (s_requests, zt_requests, z_requests, d_requests)]
    asks = exchange_asks(jnp.concatenate(wanted, axis=1))
    pairs = [
        jnp.where(pair < 0, peers, standing(jnp.maximum(pair, 0), peers)) for pair in (y_pairs, d_pairs, e_pairs, z_pairs)
    ]
    s_own = s_blocks.reshape(flat_shape)
    z_own = z_blocks.reshape(flat_shape)
    z_other = from_partner(z_own)
    first = pick(asks, (s_own, z_own, z_other), ((0, 0, 1), (1, 1, 3)), "pick_s_zt")
    second = pick(asks, (z_own, z_other), ((2, 0, 2),), "pick_z")
    first = exchange(first)
    first, second = lax.optimization_barrier((first, second))
    z_fetched = exchange(second)
    make_d = functools.partial(yd_kernel, (0, 1))
    d_blocks = paired_call(make_d, "make_d", pairs[:2], (first,), (z_blocks,))
    d_own = d_blocks.reshape(flat_shape)
    d_other = from_partner(d_own)
    third = pick(asks, (d_own, d_other), ((3, 0, 2),), "pick_d")
    d_fetched = exchange(third)
    refine = functools.partial(ez_kernel, (0, 0))
    return paired_call(refine, "refine", pairs[2:], (d_fetched, z_fetched), (d_blocks, z_blocks))


def solution(mesh):
    blocks = P(("leaf", "col"), None, None, None)
    requests = P("leaf", "col", None, None)
    pairs = P(("leaf", "col"), None, None)
    in_specs = (blocks, blocks) + (requests, pairs) * 4
    return jax.shard_map(on_device, mesh=mesh, in_specs=in_specs, out_specs=blocks, check_vma=False)
```

```python
import functools

import jax
import jax.numpy as jnp
from jax import lax
from jax.experimental import pallas as pl
from jax.experimental.pallas import tpu as pltpu
from jax.sharding import PartitionSpec as P

BF16 = jnp.bfloat16
F32 = jnp.float32
SMEM = pl.BlockSpec(memory_space=pltpu.SMEM)
VMEM = pl.BlockSpec(memory_space=pltpu.VMEM)
ANY = pl.BlockSpec(memory_space=pl.ANY)


def from_partner(value):
    pairs = [(source, source ^ 1) for source in range(lax.axis_size("leaf"))]
    return lax.ppermute(value, "leaf", pairs)


def first_of(count):
    return count // 2 + 5


def standing(peer, count):
    return (first_of(count) - peer + count) % count


def exchange(value):
    count = lax.axis_size("col")
    group = sorted(range(count), key=lambda peer: standing(peer, count))
    return lax.all_to_all(value, "col", 0, 0, axis_index_groups=[group], tiled=True)


def turned(count):
    return 2 * (count // 3) + 2


def exchange_asks(asks):
    count = asks.shape[0]
    group = [(row + turned(count)) % count for row in range(count)]
    asks = jnp.roll(asks, -turned(count), axis=0)
    return lax.all_to_all(asks, "col", 0, 0, axis_index_groups=[group], tiled=True)


def asks_row(place, count):
    row = (first_of(count) - turned(count)) % count - place
    return jnp.where(row < 0, row + count, row)


def pick_kernel(lists, asks, *refs):
    sources = max(end for _, _, end in lists)
    held, out = refs[:sources], refs[sources]
    stores, asked, sem, in_sems = refs[sources + 1 : -3], refs[-3], refs[-2], refs[-1]
    readers = out.shape[0]
    ask_copy = pltpu.make_async_copy(asks, asked, in_sems.at[in_sems.shape[0] - 1])
    ask_copy.start()
    loads, sizes = [], []
    for store, (_, begin, end) in zip(stores, lists):
        first, mine = 0, []
        for h in range(begin, end):
            count = held[h].shape[0]
            load_sem = in_sems.at[sum(map(len, loads)) + len(mine)]
            mine.append(pltpu.make_async_copy(held[h], store.at[pl.ds(first, count)], load_sem))
            first += count
        loads.append(mine)
        sizes.append(first)
    for mine in loads:
        for load in mine:
            load.start()
    for store, size in zip(stores, sizes):
        store[size] = jnp.zeros(store.shape[1:], BF16)
    ask_copy.wait()
    for place, (store, size, mine, (row, _, _)) in enumerate(zip(stores, sizes, loads, lists)):
        for load in mine:
            load.wait()

        @pl.loop(0, readers)
        def _(reader):
            slot = asked[asks_row(reader, readers), row]
            at = jnp.where(slot < 0, size, slot)
            pltpu.make_async_copy(store.at[at], out.at[reader, place], sem).start()

    pltpu.make_async_copy(out, out, sem).wait()


def pick(asks, holdings, lists, name):
    block = holdings[0].shape[1:]
    shape = (asks.shape[0], len(lists)) + block
    size = 2 * shape[0] * shape[1] * shape[2] * shape[3]
    stores = [
        pltpu.VMEM((1 + sum(h.shape[0] for h in holdings[begin:end]),) + block, BF16) for _, begin, end in lists
    ]
    return pl.pallas_call(
        functools.partial(pick_kernel, lists),
        out_shape=jax.ShapeDtypeStruct(shape, BF16),
        in_specs=[ANY] * (1 + len(holdings)),
        out_specs=ANY,
        scratch_shapes=[
            *stores,
            pltpu.SMEM(asks.shape, jnp.int32),
            pltpu.SemaphoreType.DMA,
            pltpu.SemaphoreType.DMA((1 + sum(end - begin for _, begin, end in lists),)),
        ],
        cost_estimate=pl.CostEstimate(flops=0, bytes_accessed=3 * size, transcendentals=0),
        name=name,
    )(asks, *holdings)


def product(pairs, blocks, g, a, right):
    chosen = [blocks[pairs[g, a, b]] for b in range(pairs.shape[2])]
    tall = right.reshape(right.shape[0] * right.shape[1], right.shape[2])
    return jnp.dot(jnp.concatenate(chosen, axis=1), tall, preferred_element_type=F32)


def yd_kernel(at, y_pairs, d_pairs, fetched, z, d, s_in, zt_in, y, sems):
    count = fetched.shape[0]
    columns, slots, size = z.shape[:3]
    copies = [
        pltpu.make_async_copy(fetched.at[:, i], into.at[pl.ds(0, count)], sems.at[i])
        for i, into in zip(at, (s_in, zt_in))
    ]
    for copy in copies:
        copy.start()
    s_in[count] = jnp.zeros((size, size), BF16)
    zt_in[count] = jnp.zeros((size, size), BF16)
    copies[0].wait()
    for g in range(columns):
        for a in range(slots):
            y[g, a] = product(y_pairs, s_in, g, a, z[g]).astype(BF16)
    copies[1].wait()

    @pl.loop(0, count)
    def _(i):
        zt_in[i] = zt_in[i].T

    rows = lax.broadcasted_iota(jnp.int32, (size, size), 0)
    identity = jnp.where(rows == lax.broadcasted_iota(jnp.int32, (size, size), 1), 1.0, 0.0)
    for g in range(columns):
        for a in range(slots):
            total = product(d_pairs, zt_in, g, a, y[g])
            d[g, a] = (identity - total if a == 0 else -total).astype(BF16)


def ez_kernel(at, e_pairs, z_pairs, d_fetched, z_fetched, d, z, out, d_in, z_in, e, sems):
    count = d_fetched.shape[0]
    columns, slots, size = z.shape[:3]
    copies = [
        pltpu.make_async_copy(src.at[:, i], into.at[pl.ds(0, count)], sems.at[k])
        for k, (i, src, into) in enumerate(zip(at, (d_fetched, z_fetched), (d_in, z_in)))
    ]
    for copy in copies:
        copy.start()
    d_in[count] = jnp.zeros((size, size), BF16)
    z_in[count] = jnp.zeros((size, size), BF16)
    copies[0].wait()
    for g in range(columns):
        for a in range(slots):
            square = product(e_pairs, d_in, g, a, d[g])
            e[g, a] = (0.5 * d[g, a].astype(F32) + 0.375 * square).astype(BF16)
    copies[1].wait()
    for g in range(columns):
        for a in range(slots):
            total = z[g, a].astype(F32) + product(z_pairs, z_in, g, a, e[g])
            out[g, a] = total.astype(BF16)


def paired_call(body, name, pairs, fetched, local):
    columns, slots, size = local[0].shape[:3]
    count = fetched[0].shape[0]
    flops = 4 * columns * slots * slots * size**3
    return pl.pallas_call(
        body,
        out_shape=jax.ShapeDtypeStruct(local[0].shape, BF16),
        in_specs=[SMEM] * 2 + [ANY] * len(fetched) + [VMEM] * len(local),
        out_specs=VMEM,
        scratch_shapes=[
            pltpu.VMEM((count + 1, size, size), BF16),
            pltpu.VMEM((count + 1, size, size), BF16),
            pltpu.VMEM(local[0].shape, BF16),
            pltpu.SemaphoreType.DMA((2,)),
        ],
        compiler_params=pltpu.CompilerParams(vmem_limit_bytes=32 * 2**20),
        cost_estimate=pl.CostEstimate(flops=flops, bytes_accessed=16 * 2**20, transcendentals=0),
        name=name,
    )(*pairs, *fetched, *local)


def on_device(
    s_blocks, z_blocks, s_requests, y_pairs, zt_requests, d_pairs, d_requests, e_pairs, z_requests, z_pairs
):
    flat_shape = (-1,) + z_blocks.shape[2:]
    peers = s_requests.shape[2]
    wanted = [r.reshape(peers, 1) for r in (s_requests, zt_requests, z_requests, d_requests)]
    asks = exchange_asks(jnp.concatenate(wanted, axis=1))
    pairs = [
        jnp.where(pair < 0, peers, standing(jnp.maximum(pair, 0), peers)) for pair in (y_pairs, d_pairs, e_pairs, z_pairs)
    ]
    s_own = s_blocks.reshape(flat_shape)
    z_own = z_blocks.reshape(flat_shape)
    z_other = from_partner(z_own)
    first = pick(asks, (s_own, z_own, z_other), ((0, 0, 1), (1, 1, 3)), "pick_s_zt")
    second = pick(asks, (z_own, z_other), ((2, 0, 2),), "pick_z")
    first = exchange(first)
    first, second = lax.optimization_barrier((first, second))
    z_fetched = exchange(second)
    make_d = functools.partial(yd_kernel, (0, 1))
    d_blocks = paired_call(make_d, "make_d", pairs[:2], (first,), (z_blocks,))
    d_own = d_blocks.reshape(flat_shape)
    d_other = from_partner(d_own)
    third = pick(asks, (d_own, d_other), ((3, 0, 2),), "pick_d")
    d_fetched = exchange(third)
    refine = functools.partial(ez_kernel, (0, 0))
    return paired_call(refine, "refine", pairs[2:], (d_fetched, z_fetched), (d_blocks, z_blocks))


def solution(mesh):
    blocks = P(("leaf", "col"), None, None, None)
    requests = P("leaf", "col", None, None)
    pairs = P(("leaf", "col"), None, None)
    in_specs = (blocks, blocks) + (requests, pairs) * 4
    return jax.shard_map(on_device, mesh=mesh, in_specs=in_specs, out_specs=blocks, check_vma=False)
```
